32 devices in a mesh: groups: 2 (over x), expert: 16 (over z, y, core).
Axes of the slice: x: 2, y: 2, z: 4, core: 2. Of those that a mesh axis runs over, the one named last changes fastest.
Arguments:
- tokens: bfloat16 [4096, 7168], P(('groups', 'expert')), parts along dimension 0, may hold values from -6 to 6
- out_grad: bfloat16 [4096, 7168], P(('groups', 'expert')), parts along dimension 0, may hold values from -6 to 6
- expert_ids: int32 [4096, 8], P(('groups', 'expert')), parts along dimension 0, may hold values from 0 to 255, as said below
- gate_weights: float32 [4096, 8], P(('groups', 'expert')), parts along dimension 0, may hold values from 0.05 to 1
- w_gate: bfloat16 [16, 7168, 256], P('expert'), may hold values from -0.0625 to 0.0625
- w_up: bfloat16 [16, 7168, 256], P('expert'), may hold values from -0.0625 to 0.0625
- in_proj: bfloat16 [16, 256, 64], P('expert'), may hold values from -0.125 to 0.125
- out_proj: bfloat16 [7168, 64], replicated, may hold values from -0.0625 to 0.0625
Outputs:
- example_grads: float32 [256, 256], P(('groups', 'expert')), parts along dimension 0
The draws below stay inside these ranges and needn't reach their ends.
There are 2 independent parts, one for each index of `groups`. The reference program is written for one: setup_inputs(seed, part) draws one part's arguments, and reference() takes and returns one part's arrays. A program takes and returns all parts, laid end to end along the dimension named above; an argument that names none is the same for every part. Nothing has to cross between parts.
Inputs may be any that keep to these rules, and one draw needn't show every extreme that they name: `expert_ids`: each row names 8 different experts. Among the 128 rows of one device every expert is named by 8, 4 or 2 rows (a quarter, a quarter and a half of the experts); one expert below 2 is named by 8 rows of every device.
All inputs are finite; a program needn't handle non-finite values.
Results may differ from the reference program's by a relative error of at most 0.0041.
Values may be sent and summed in bfloat16 or wider, within the bound.
A program may use at most 128 MiB of HBM per device.

```python
import math
import jax
import jax.numpy as jnp
from jax import lax

D = 7168
EXPERT_FF = 2048
EXPERTS_ALL = 256
TOPK = 8
R = 64
STRIPES = 8
TOK_DEV = 128
TOKENS = 2048
FLIGHT = 2
HS = 256
CAPACITY = 8
EXAMPLES = 4


def draw_expert_ids(key, part):
    key = jax.random.fold_in(key, 11)
    blocks = TOKENS // TOK_DEV
    listing = jnp.arange(EXPERTS_ALL, dtype=jnp.int32)
    quarter = EXPERTS_ALL // 4
    levels = jnp.where(listing < quarter, CAPACITY, jnp.where(listing < 2 * quarter, CAPACITY // 2, CAPACITY // 4)).astype(jnp.int32)
    favored = jax.random.randint(jax.random.fold_in(key, 1), (), 0, FLIGHT).astype(jnp.int32)

    def one_block(block_key):
        order_key, shuffle_key = jax.random.split(block_key)
        shuffled = jax.random.permutation(order_key, EXPERTS_ALL).astype(jnp.int32)
        here = shuffled[favored]
        places = jnp.where(listing == favored, 0, jnp.where(shuffled == 0, here, shuffled))
        counts = levels[places]
        listed = jnp.repeat(listing, counts, total_repeat_length=TOK_DEV * TOPK)
        table = listed.reshape(TOPK, TOK_DEV).T
        rowperm = jax.random.permutation(shuffle_key, TOK_DEV)
        return table[rowperm]
    keys = jax.random.split(jax.random.fold_in(key, 2), blocks)
    return jax.vmap(one_block)(keys).reshape(TOKENS, TOPK).astype(jnp.int32)


def shard_levels(key, extent, cuts, least, largest):
    factor_of = 1.0
    for position, parts in cuts:
        draws = jax.random.uniform(jax.random.fold_in(jax.random.fold_in(key, 6), position), (parts,), jnp.float32, least / len(cuts), largest / len(cuts))
        factor_of = factor_of * jnp.repeat(jnp.exp(draws), extent[position] // parts).reshape((-1,) + (1,) * (len(extent) - 1 - position))
    return factor_of


def centred(own_key, shape, spread, bound, cuts=(), kind=jnp.bfloat16):
    values = jax.random.normal(own_key, shape, jnp.float32) * spread
    if len(cuts) > 0:
        values = shard_levels(own_key, shape, cuts, -0.22, 0.18) * values
    return jnp.clip(values, min=-bound, max=bound).astype(kind)


def setup_inputs(seed: int = 0, part: int = 0) -> dict:
    seeds = jax.random.split(jax.random.key(seed), 9)
    part_splits = jax.random.split(jax.random.fold_in(seeds[8], part), 9)
    tokens = centred(part_splits[0], (TOKENS, D), 1.0, 6.0, ((0, 16),))
    out_grad = centred(part_splits[1], (TOKENS, D), 1.0, 6.0, ((0, 16),))
    expert_ids = draw_expert_ids(jax.random.fold_in(jax.random.fold_in(seeds[8], part), 71), part)
    gate_weights = jnp.clip(jnp.exp(math.log(1.0) - 2.9957323 * jax.random.uniform(part_splits[3], (TOKENS, TOPK), jnp.float32) ** shard_levels(part_splits[3], (TOKENS, TOPK), ((0, 16),), -0.2, 0.2)), 0.05, 1.0)
    w_gate = centred(seeds[4], (FLIGHT * STRIPES, D, HS), D ** -0.5, 0.0625, ((0, 16),))
    w_up = centred(seeds[5], (FLIGHT * STRIPES, D, HS), D ** -0.5, 0.0625, ((0, 16),))
    in_proj = centred(seeds[6], (FLIGHT * STRIPES, HS, R), EXPERT_FF ** -0.5, 0.125, ((0, 16),))
    out_proj = centred(seeds[7], (D, R), D ** -0.5, 0.0625)
    return dict(tokens=tokens, out_grad=out_grad, expert_ids=expert_ids, gate_weights=gate_weights, w_gate=w_gate, w_up=w_up, in_proj=in_proj, out_proj=out_proj)


def reference(tokens, out_grad, expert_ids, gate_weights, w_gate, w_up, in_proj, out_proj):
    blocks = TOKENS // TOK_DEV
    slots = blocks * CAPACITY
    projected = jnp.dot(out_grad, out_proj, preferred_element_type=jnp.float32)
    token_index = jnp.arange(TOKENS, dtype=jnp.int32)

    def one_expert(expert):
        matches = expert_ids == expert
        weight = jnp.sum(jnp.where(matches, gate_weights, jnp.zeros_like(gate_weights)), axis=1)
        routed = jnp.any(matches, axis=1).astype(jnp.int32)
        ranks = jnp.cumsum(routed.reshape(blocks, TOK_DEV), axis=1).reshape(TOKENS) - 1
        target = jnp.where(routed == 1, (token_index // TOK_DEV) * CAPACITY + ranks, slots).astype(jnp.int32)
        rows = jnp.zeros((slots,), jnp.int32).at[target].set(token_index, mode="drop")
        filled = jnp.zeros((slots,), jnp.int32).at[target].set(1, mode="drop")
        weighted = (weight[:, None] * projected).astype(jnp.bfloat16)
        grads = jnp.where(filled[:, None] == 1, weighted[rows], jnp.zeros((), jnp.bfloat16))
        chosen = tokens[rows]
        start = (expert * STRIPES).astype(jnp.int32)
        gate_cols = jnp.transpose(lax.dynamic_slice_in_dim(w_gate, start, STRIPES, 0), (1, 0, 2)).reshape(D, EXPERT_FF)
        up_cols = jnp.transpose(lax.dynamic_slice_in_dim(w_up, start, STRIPES, 0), (1, 0, 2)).reshape(D, EXPERT_FF)
        proj_rows = lax.dynamic_slice_in_dim(in_proj, start, STRIPES, 0).reshape(EXPERT_FF, R)
        gate = jnp.dot(chosen, gate_cols, preferred_element_type=jnp.float32)
        up = jnp.dot(chosen, up_cols, preferred_element_type=jnp.float32)
        hidden = (jax.nn.silu(gate) * up).astype(jnp.bfloat16)
        inputs = jnp.dot(hidden, proj_rows, preferred_element_type=jnp.float32)
        inputs = inputs.reshape(EXAMPLES, slots // EXAMPLES, R)
        grads = grads.astype(jnp.float32).reshape(EXAMPLES, slots // EXAMPLES, R)
        outer = jnp.einsum("bmi,bmj->ibj", grads, inputs, precision=lax.Precision.HIGHEST)
        return outer.reshape(R, EXAMPLES * R)

    result = lax.map(one_expert, jnp.arange(FLIGHT, dtype=jnp.int32))
    return result.reshape(FLIGHT * R, EXAMPLES * R)
```

```python
import functools
import jax
import jax.numpy as jnp
from jax import lax
from jax.experimental import pallas as pl
from jax.experimental.pallas import tpu as pltpu
from jax.sharding import PartitionSpec as P

STRIPES = 8
EX_LEN = 512
CAPACITY = 8
HALVES = 2
GROUP = 16
BF16 = jnp.bfloat16
F32 = jnp.float32


def toggled(m, bit):
    size = 1 << bit
    return m + size - 2 * size * lax.rem(lax.div(m, size), 2)


def kernel(
    n,
    tokens,
    out_grad,
    ids_hbm,
    gates_hbm,
    w_gate,
    w_up,
    in_proj,
    out_proj,
    out,
    tok,
    og,
    ids,
    gw,
    wg,
    wu,
    ip,
    op,
    outgoing,
    rows,
    grads_out,
    grads_in,
    sums_out,
    sums_in,
    load_sem,
    local_sem,
    send_sem,
    recv_sem,
    gsend_sem,
    grecv_sem,
    ssend_sem,
    srecv_sem,
):
    flight = n // STRIPES
    me = lax.axis_index("expert")
    octet, member = lax.div(me, STRIPES), lax.rem(me, STRIPES)
    base = octet * STRIPES
    width = tok.shape[1]
    tok_rows = tok.shape[0]
    rank = op.shape[1]
    part = rows.shape[3]

    loads = [
        pltpu.make_async_copy(src, dst, load_sem.at[i])
        for i, (src, dst) in enumerate(
            (
                (ids_hbm, ids),
                (gates_hbm, gw),
                (tokens, tok),
                (out_grad, og),
                (out_proj, op),
                (in_proj.at[0], ip),
                (w_gate.at[0], wg),
                (w_up.at[0], wu),
            )
        )
    ]
    for load in loads:
        load.start()

    barrier = pltpu.get_barrier_semaphore()

    def greet(step, carry):
        pl.semaphore_signal(barrier, inc=1, device_id={"expert": lax.rem(me + step, n)})
        return carry

    lax.fori_loop(1, n, greet, 0)

    loads[0].wait()
    loads[1].wait()
    lanes = max(128, flight * CAPACITY)
    lane = lax.broadcasted_iota(jnp.int32, (tok_rows, lanes), 1)
    expert_of, slot_of = lax.div(lane, CAPACITY), lax.rem(lane, CAPACITY)
    routed = jnp.zeros((tok_rows, lanes), F32)
    weight = jnp.zeros((tok_rows, lanes), F32)
    for k in range(ids.shape[1]):
        match = ids[:, k : k + 1] == expert_of
        routed = jnp.where(match, 1.0, routed)
        weight = weight + jnp.where(match, gw[:, k : k + 1], 0.0)
    below = lax.broadcasted_iota(jnp.int32, (tok_rows, tok_rows), 0) >= lax.broadcasted_iota(
        jnp.int32, (tok_rows, tok_rows), 1
    )
    ranks = jnp.dot(
        jnp.where(below, 1.0, 0.0).astype(BF16), routed.astype(BF16), preferred_element_type=F32
    )
    taken = (routed > 0.0) & (ranks == (slot_of + 1).astype(F32))
    used = flight * CAPACITY
    sel = jnp.where(taken, 1.0, 0.0).T[:used].astype(BF16)
    slot_weight = jnp.sum(jnp.where(taken, weight, 0.0).T[:used], axis=1, keepdims=True)

    loads[2].wait()
    half = width // 2
    for h in range(HALVES):
        lo = h * part
        left = jnp.dot(sel, tok[:, lo : lo + part], preferred_element_type=F32)
        right = jnp.dot(sel, tok[:, half + lo : half + lo + part], preferred_element_type=F32)
        for e in range(flight):
            at = slice(e * CAPACITY, (e + 1) * CAPACITY)
            outgoing[h, e] = jnp.concatenate([left[at], right[at]], axis=0).astype(BF16)

    pl.semaphore_wait(barrier, n - 1)

    def send(src, source, h, target):
        pltpu.make_async_remote_copy(
            src_ref=src,
            dst_ref=rows.at[h, source],
            send_sem=send_sem,
            recv_sem=recv_sem.at[h, source],
            device_id={"expert": target},
        ).start()

    def arrived(source, h):
        pltpu.make_async_copy(
            rows.at[h, source], rows.at[h, source], recv_sem.at[h, source]
        ).wait()

    core, near, far = (base + toggled(member, bit) for bit in range(3))

    def across(step, carry):
        e = lax.rem(octet + step, flight)
        for h in range(HALVES):
            send(outgoing.at[h, e], me, h, e * STRIPES + member)
        return carry

    lax.fori_loop(1, flight, across, 0)
    own = []
    for h in range(HALVES):
        for target in (far, near, core):
            send(outgoing.at[h, octet], me, h, target)
        keep = pltpu.make_async_copy(outgoing.at[h, octet], rows.at[h, me], local_sem.at[h])
        keep.start()
        own.append(keep)

    loads[3].wait()
    loads[4].wait()
    chosen = jnp.dot(sel, og[...], preferred_element_type=F32).astype(BF16)
    projected = jnp.dot(chosen, op[...], preferred_element_type=F32)
    weighted = (slot_weight * projected).astype(BF16).astype(F32)
    weighted = jnp.concatenate([weighted, jnp.zeros_like(weighted)], axis=1)
    for e in range(flight):
        grads_out[e] = weighted[e * CAPACITY : (e + 1) * CAPACITY]

    def send_grads(step, carry):
        target = lax.rem(me + step, n)
        pltpu.make_async_remote_copy(
            src_ref=grads_out.at[lax.div(target, STRIPES)],
            dst_ref=grads_in.at[me],
            send_sem=gsend_sem,
            recv_sem=grecv_sem,
            device_id={"expert": target},
        ).start()
        return carry

    lax.fori_loop(1, n, send_grads, 0)
    grads_in[me] = grads_out[octet]

    def spread(at):
        near_source, far_source = at + toggled(member, 1), at + toggled(member, 2)
        arrived(far_source, 1)
        send(rows.at[1, far_source], far_source, 1, near)
        send(rows.at[1, far_source], far_source, 1, core)
        arrived(near_source, 0)
        send(rows.at[0, near_source], near_source, 0, far)
        send(rows.at[0, near_source], near_source, 0, core)
        arrived(near_source, 1)
        send(rows.at[1, near_source], near_source, 1, core)
        arrived(far_source, 0)
        send(rows.at[0, far_source], far_source, 0, core)

    def finish(at):
        diagonal = at + toggled(toggled(member, 1), 2)
        for h in range(HALVES):
            arrived(diagonal, h)
            send(rows.at[h, diagonal], diagonal, h, core)

    def settle(at):
        for bits in ((), (1,), (2,), (1, 2)):
            source = toggled(member, 0)
            for bit in bits:
                source = toggled(source, bit)
            for h in range(HALVES):
                arrived(at + source, h)

    spread(base)

    def onward(step, carry):
        at = lax.rem(octet + step, flight) * STRIPES
        for h in (1, 0):
            arrived(at + member, h)
            for target in (far, near, core):
                send(rows.at[h, at + member], at + member, h, target)
        return carry

    lax.fori_loop(1, flight, onward, 0)
    finish(base)

    def rest(step, carry):
        at = lax.rem(octet + step, flight) * STRIPES
        spread(at)
        finish(at)
        return carry

    lax.fori_loop(1, flight, rest, 0)

    loads[5].wait()
    examples_each = GROUP * tok_rows // EX_LEN
    cols = examples_each * rank
    repeat = jnp.where(
        lax.rem(lax.broadcasted_iota(jnp.int32, (rank, cols), 1), rank)
        == lax.broadcasted_iota(jnp.int32, (rank, cols), 0),
        1.0,
        0.0,
    ).astype(BF16)
    ip_wide = jnp.dot(ip[...], repeat, preferred_element_type=F32).astype(BF16)
    loads[6].wait()
    loads[7].wait()

    def settled(step, carry):
        settle(step * STRIPES)
        return carry

    lax.fori_loop(0, flight, settled, 0)
    for keep in own:
        keep.wait()
    pltpu.make_async_copy(
        grads_in.at[pl.ds(0, n - 1)], grads_in.at[pl.ds(0, n - 1)], grecv_sem
    ).wait()

    count = GROUP * CAPACITY
    keep_cols = lax.div(
        lax.broadcasted_iota(jnp.int32, (count, cols), 0), EX_LEN // tok_rows * CAPACITY
    ) == lax.div(lax.broadcasted_iota(jnp.int32, (count, cols), 1), rank)

    def block(g, carry):
        sources = pl.ds(pl.multiple_of(g * GROUP, GROUP), GROUP)
        gate = jnp.zeros((count, wg.shape[1]), F32)
        up = jnp.zeros((count, wg.shape[1]), F32)
        for h in range(HALVES):
            both = rows[h, sources].astype(F32)
            for side in range(2):
                x = both[:, side * CAPACITY : (side + 1) * CAPACITY].reshape(count, part)
                x = x.astype(BF16)
                lo = side * half + h * part
                gate = gate + jnp.dot(x, wg[lo : lo + part], preferred_element_type=F32)
                up = up + jnp.dot(x, wu[lo : lo + part], preferred_element_type=F32)
        hidden = (gate / (1.0 + jnp.exp(-gate)) * up).astype(BF16)
        inputs = jnp.dot(hidden, ip_wide, preferred_element_type=F32)
        inputs = jnp.where(keep_cols, inputs, 0.0)
        high = inputs.astype(BF16)
        rest_of = inputs - high.astype(F32)
        mid = rest_of.astype(BF16)
        low = (rest_of - mid.astype(F32)).astype(BF16)
        g_rows = grads_in[sources].reshape(count, grads_in.shape[2]).astype(BF16)
        contract = (((0,), (0,)), ((), ()))
        total = lax.dot_general(
            jnp.concatenate([g_rows, g_rows, g_rows], axis=0),
            jnp.concatenate([low, mid, high], axis=0),
            contract,
            preferred_element_type=F32,
        )
        sums_out[:, :, pl.ds(pl.multiple_of(g * cols, cols), cols)] = total[:rank].reshape(
            STRIPES, rank // STRIPES, cols
        )
        return carry

    lax.fori_loop(0, n // GROUP, block, 0)

    for step in range(1, STRIPES):
        target = lax.rem(member + step, STRIPES)
        pltpu.make_async_remote_copy(
            src_ref=sums_out.at[target],
            dst_ref=sums_in.at[member],
            send_sem=ssend_sem,
            recv_sem=srecv_sem,
            device_id={"expert": base + target},
        ).start()
    sums_in[member] = sums_out[member]
    others = pl.ds(0, STRIPES - 1)
    pltpu.make_async_copy(
        rows.at[:, pl.ds(0, n - 1)], rows.at[:, pl.ds(0, n - 1)], send_sem
    ).wait()
    pltpu.make_async_copy(
        grads_in.at[pl.ds(0, n - 1)], grads_in.at[pl.ds(0, n - 1)], gsend_sem
    ).wait()
    pltpu.make_async_copy(sums_in.at[others], sums_in.at[others], srecv_sem).wait()
    total = sums_in[0]
    for j in range(1, STRIPES):
        total = total + sums_in[j]
    out[...] = total
    pltpu.make_async_copy(sums_in.at[others], sums_in.at[others], ssend_sem).wait()


def on_device(tokens, out_grad, expert_ids, gate_weights, w_gate, w_up, in_proj, out_proj):
    n = lax.axis_size("expert")
    flight = n // STRIPES
    tok_rows, width = tokens.shape
    hidden_units = w_gate.shape[2]
    rank = out_proj.shape[1]
    part = width // 2 // HALVES
    out_cols = n * tok_rows // EX_LEN * rank
    rank_each = rank // STRIPES
    dma = pltpu.SemaphoreType.DMA
    return pl.pallas_call(
        functools.partial(kernel, n),
        out_shape=jax.ShapeDtypeStruct((rank_each, out_cols), F32),
        in_specs=[pl.BlockSpec(memory_space=pl.ANY)] * 8,
        out_specs=pl.BlockSpec(memory_space=pltpu.VMEM),
        scratch_shapes=[
            pltpu.VMEM((tok_rows, width), BF16),
            pltpu.VMEM((tok_rows, width), BF16),
            pltpu.VMEM(expert_ids.shape, jnp.int32),
            pltpu.VMEM(gate_weights.shape, F32),
            pltpu.VMEM((width, hidden_units), BF16),
            pltpu.VMEM((width, hidden_units), BF16),
            pltpu.VMEM((hidden_units, rank), BF16),
            pltpu.VMEM((width, rank), BF16),
            pltpu.VMEM((HALVES, flight, 2 * CAPACITY, part), BF16),
            pltpu.VMEM((HALVES, n, 2 * CAPACITY, part), BF16),
            pltpu.VMEM((flight, CAPACITY, 2 * rank), F32),
            pltpu.VMEM((n, CAPACITY, 2 * rank), F32),
            pltpu.VMEM((STRIPES, rank_each, out_cols), F32),
            pltpu.VMEM((STRIPES, rank_each, out_cols), F32),
            dma((8,)),
            dma((HALVES,)),
            dma,
            dma((HALVES, n)),
            dma,
            dma,
            dma,
            dma,
        ],
        compiler_params=pltpu.CompilerParams(
            collective_id=0, has_side_effects=True, vmem_limit_bytes=56 * 1024 * 1024
        ),
    )(tokens, out_grad, expert_ids, gate_weights, w_gate, w_up, in_proj, out_proj)


def solution(mesh):
    placed = (
        P(("groups", "expert"), None),
        P(("groups", "expert"), None),
        P(("groups", "expert"), None),
        P(("groups", "expert"), None),
        P("expert", None, None),
        P("expert", None, None),
        P("expert", None, None),
        P(),
    )
    return jax.shard_map(
        on_device,
        mesh=mesh,
        in_specs=placed,
        out_specs=P(("groups", "expert"), None),
        check_vma=False,
    )
```

```python
import functools
import jax
import jax.numpy as jnp
from jax import lax
from jax.experimental import pallas as pl
from jax.experimental.pallas import tpu as pltpu
from jax.sharding import PartitionSpec as P

STRIPES = 8
EX_LEN = 512
CAPACITY = 8
HALVES = 2
GROUP = 16
BF16 = jnp.bfloat16
F32 = jnp.float32
BY_LAST = (((1,), (1,)), ((), ()))


def toggled(m, bit):
    size = 1 << bit
    return m + size - 2 * size * lax.rem(lax.div(m, size), 2)


def kernel(
    n,
    tokens,
    out_grad,
    ids_hbm,
    gates_hbm,
    w_gate,
    w_up,
    in_proj,
    out_proj,
    out,
    tok,
    og,
    ids,
    gw,
    wg,
    wu,
    ip,
    op,
    outgoing,
    rows,
    grads_out,
    grads_in,
    sums_out,
    sums_in,
    load_sem,
    local_sem,
    send_sem,
    recv_sem,
    gsend_sem,
    grecv_sem,
    ssend_sem,
    srecv_sem,
):
    flight = n // STRIPES
    me = lax.axis_index("expert")
    octet, member = lax.div(me, STRIPES), lax.rem(me, STRIPES)
    base = octet * STRIPES
    width = tok.shape[1]
    tok_rows = tok.shape[0]
    rank = op.shape[0]
    part = rows.shape[3]

    loads = [
        pltpu.make_async_copy(src, dst, load_sem.at[i])
        for i, (src, dst) in enumerate(
            (
                (ids_hbm, ids),
                (gates_hbm, gw),
                (tokens, tok),
                (out_grad, og),
                (out_proj, op),
                (in_proj.at[0], ip),
                (w_gate.at[0], wg),
                (w_up.at[0], wu),
            )
        )
    ]
    for load in loads:
        load.start()

    barrier = pltpu.get_barrier_semaphore()

    def greet(step, carry):
        pl.semaphore_signal(barrier, inc=1, device_id={"expert": lax.rem(me + step, n)})
        return carry

    lax.fori_loop(1, n, greet, 0)

    loads[0].wait()
    loads[1].wait()
    used = flight * CAPACITY
    line = lax.broadcasted_iota(jnp.int32, (used, tok_rows), 0)
    expert_of, slot_of = lax.div(line, CAPACITY), lax.rem(line, CAPACITY)
    routed = jnp.zeros((used, tok_rows), F32)
    weight = jnp.zeros((used, tok_rows), F32)
    for k in range(ids.shape[0]):
        match = ids[k : k + 1] == expert_of
        routed = jnp.where(match, 1.0, routed)
        weight = weight + jnp.where(match, gw[k : k + 1], 0.0)
    upto = lax.broadcasted_iota(jnp.int32, (tok_rows, tok_rows), 0) <= lax.broadcasted_iota(
        jnp.int32, (tok_rows, tok_rows), 1
    )
    ranks = jnp.dot(
        routed.astype(BF16), jnp.where(upto, 1.0, 0.0).astype(BF16), preferred_element_type=F32
    )
    taken = (routed > 0.0) & (ranks == (slot_of + 1).astype(F32))
    sel = jnp.where(taken, 1.0, 0.0).astype(BF16)
    slot_weight = jnp.sum(jnp.where(taken, weight, 0.0), axis=1, keepdims=True)

    loads[2].wait()
    half = width // 2
    for h in range(HALVES):
        lo = h * part
        left = jnp.dot(sel, tok[:, lo : lo + part], preferred_element_type=F32)
        right = jnp.dot(sel, tok[:, half + lo : half + lo + part], preferred_element_type=F32)
        for e in range(flight):
            at = slice(e * CAPACITY, (e + 1) * CAPACITY)
            outgoing[h, e] = jnp.concatenate([left[at], right[at]], axis=0).astype(BF16)

    pl.semaphore_wait(barrier, n - 1)

    def send(src, source, h, target):
        pltpu.make_async_remote_copy(
            src_ref=src,
            dst_ref=rows.at[h, source],
            send_sem=send_sem,
            recv_sem=recv_sem.at[h, source],
            device_id={"expert": target},
        ).start()

    def arrived(source, h):
        pltpu.make_async_copy(
            rows.at[h, source], rows.at[h, source], recv_sem.at[h, source]
        ).wait()

    core, near, far = (base + toggled(member, bit) for bit in range(3))

    def across(step, carry):
        e = lax.rem(octet + step, flight)
        for h in range(HALVES):
            send(outgoing.at[h, e], me, h, e * STRIPES + member)
        return carry

    lax.fori_loop(1, flight, across, 0)
    own = []
    for h in range(HALVES):
        for target in (far, near, core):
            send(outgoing.at[h, octet], me, h, target)
        keep = pltpu.make_async_copy(outgoing.at[h, octet], rows.at[h, me], local_sem.at[h])
        keep.start()
        own.append(keep)

    loads[3].wait()
    loads[4].wait()
    chosen = jnp.dot(sel, og[...], preferred_element_type=F32).astype(BF16)
    projected = lax.dot_general(chosen, op[...], BY_LAST, preferred_element_type=F32)
    weighted = (slot_weight * projected).astype(BF16).astype(F32)
    weighted = jnp.concatenate([weighted, jnp.zeros_like(weighted)], axis=1)
    for e in range(flight):
        grads_out[e] = weighted[e * CAPACITY : (e + 1) * CAPACITY]

    def send_grads(step, carry):
        target = lax.rem(me + step, n)
        pltpu.make_async_remote_copy(
            src_ref=grads_out.at[lax.div(target, STRIPES)],
            dst_ref=grads_in.at[me],
            send_sem=gsend_sem,
            recv_sem=grecv_sem,
            device_id={"expert": target},
        ).start()
        return carry

    lax.fori_loop(1, n, send_grads, 0)
    grads_in[me] = grads_out[octet]

    def spread(at):
        near_source, far_source = at + toggled(member, 1), at + toggled(member, 2)
        arrived(far_source, 1)
        send(rows.at[1, far_source], far_source, 1, near)
        send(rows.at[1, far_source], far_source, 1, core)
        arrived(near_source, 0)
        send(rows.at[0, near_source], near_source, 0, far)
        send(rows.at[0, near_source], near_source, 0, core)
        arrived(near_source, 1)
        send(rows.at[1, near_source], near_source, 1, core)
        arrived(far_source, 0)
        send(rows.at[0, far_source], far_source, 0, core)

    def finish(at):
        diagonal = at + toggled(toggled(member, 1), 2)
        for h in range(HALVES):
            arrived(diagonal, h)
            send(rows.at[h, diagonal], diagonal, h, core)

    def settle(at):
        for bits in ((), (1,), (2,), (1, 2)):
            source = toggled(member, 0)
            for bit in bits:
                source = toggled(source, bit)
            for h in range(HALVES):
                arrived(at + source, h)

    spread(base)

    def onward(step, carry):
        at = lax.rem(octet + step, flight) * STRIPES
        for h in (1, 0):
            arrived(at + member, h)
            for target in (far, near, core):
                send(rows.at[h, at + member], at + member, h, target)
        return carry

    lax.fori_loop(1, flight, onward, 0)
    finish(base)

    def rest(step, carry):
        at = lax.rem(octet + step, flight) * STRIPES
        spread(at)
        finish(at)
        return carry

    lax.fori_loop(1, flight, rest, 0)

    loads[5].wait()
    examples_each = GROUP * tok_rows // EX_LEN
    cols = examples_each * rank
    ip_wide = jnp.concatenate([ip[...]] * examples_each, axis=0)
    loads[6].wait()
    loads[7].wait()

    def settled(step, carry):
        settle(step * STRIPES)
        return carry

    lax.fori_loop(0, flight, settled, 0)
    for keep in own:
        keep.wait()
    pltpu.make_async_copy(
        grads_in.at[pl.ds(0, n - 1)], grads_in.at[pl.ds(0, n - 1)], grecv_sem
    ).wait()

    count = GROUP * CAPACITY
    keep_cols = lax.div(
        lax.broadcasted_iota(jnp.int32, (count, cols), 0), EX_LEN // tok_rows * CAPACITY
    ) == lax.div(lax.broadcasted_iota(jnp.int32, (count, cols), 1), rank)

    def block(g, carry):
        sources = pl.ds(pl.multiple_of(g * GROUP, GROUP), GROUP)
        gate = jnp.zeros((count, wg.shape[1]), F32)
        up = jnp.zeros((count, wg.shape[1]), F32)
        for h in range(HALVES):
            both = rows[h, sources].astype(F32)
            for side in range(2):
                x = both[:, side * CAPACITY : (side + 1) * CAPACITY].reshape(count, part)
                x = x.astype(BF16)
                lo = side * half + h * part
                gate = gate + jnp.dot(x, wg[lo : lo + part], preferred_element_type=F32)
                up = up + jnp.dot(x, wu[lo : lo + part], preferred_element_type=F32)
        hidden = (gate / (1.0 + jnp.exp(-gate)) * up).astype(BF16)
        inputs = lax.dot_general(hidden, ip_wide, BY_LAST, preferred_element_type=F32)
        inputs = jnp.where(keep_cols, inputs, 0.0)
        high = inputs.astype(BF16)
        rest_of = inputs - high.astype(F32)
        mid = rest_of.astype(BF16)
        low = (rest_of - mid.astype(F32)).astype(BF16)
        g_rows = grads_in[sources].reshape(count, grads_in.shape[2]).astype(BF16)
        contract = (((0,), (0,)), ((), ()))
        total = lax.dot_general(
            jnp.concatenate([g_rows, g_rows, g_rows], axis=0),
            jnp.concatenate([low, mid, high], axis=0),
            contract,
            preferred_element_type=F32,
        )
        sums_out[:, :, pl.ds(pl.multiple_of(g * cols, cols), cols)] = total[:rank].reshape(
            STRIPES, rank // STRIPES, cols
        )
        return carry

    lax.fori_loop(0, n // GROUP, block, 0)

    for step in range(1, STRIPES):
        target = lax.rem(member + step, STRIPES)
        pltpu.make_async_remote_copy(
            src_ref=sums_out.at[target],
            dst_ref=sums_in.at[member],
            send_sem=ssend_sem,
            recv_sem=srecv_sem,
            device_id={"expert": base + target},
        ).start()
    sums_in[member] = sums_out[member]
    others = pl.ds(0, STRIPES - 1)
    pltpu.make_async_copy(
        rows.at[:, pl.ds(0, n - 1)], rows.at[:, pl.ds(0, n - 1)], send_sem
    ).wait()
    pltpu.make_async_copy(
        grads_in.at[pl.ds(0, n - 1)], grads_in.at[pl.ds(0, n - 1)], gsend_sem
    ).wait()
    pltpu.make_async_copy(sums_in.at[others], sums_in.at[others], srecv_sem).wait()
    total = sums_in[0]
    for j in range(1, STRIPES):
        total = total + sums_in[j]
    out[...] = total
    pltpu.make_async_copy(sums_in.at[others], sums_in.at[others], ssend_sem).wait()


def on_device(tokens, out_grad, expert_ids, gate_weights, w_gate, w_up, in_proj, out_proj):
    n = lax.axis_size("expert")
    flight = n // STRIPES
    tok_rows, width = tokens.shape
    hidden_units = w_gate.shape[2]
    rank = out_proj.shape[1]
    part = width // 2 // HALVES
    out_cols = n * tok_rows // EX_LEN * rank
    rank_each = rank // STRIPES
    dma = pltpu.SemaphoreType.DMA
    return pl.pallas_call(
        functools.partial(kernel, n),
        out_shape=jax.ShapeDtypeStruct((rank_each, out_cols), F32),
        in_specs=[pl.BlockSpec(memory_space=pl.ANY)] * 8,
        out_specs=pl.BlockSpec(memory_space=pltpu.VMEM),
        scratch_shapes=[
            pltpu.VMEM((tok_rows, width), BF16),
            pltpu.VMEM((tok_rows, width), BF16),
            pltpu.VMEM(expert_ids.shape[::-1], jnp.int32),
            pltpu.VMEM(gate_weights.shape[::-1], F32),
            pltpu.VMEM((width, hidden_units), BF16),
            pltpu.VMEM((width, hidden_units), BF16),
            pltpu.VMEM((rank, hidden_units), BF16),
            pltpu.VMEM((rank, width), BF16),
            pltpu.VMEM((HALVES, flight, 2 * CAPACITY, part), BF16),
            pltpu.VMEM((HALVES, n, 2 * CAPACITY, part), BF16),
            pltpu.VMEM((flight, CAPACITY, 2 * rank), F32),
            pltpu.VMEM((n, CAPACITY, 2 * rank), F32),
            pltpu.VMEM((STRIPES, rank_each, out_cols), F32),
            pltpu.VMEM((STRIPES, rank_each, out_cols), F32),
            dma((8,)),
            dma((HALVES,)),
            dma,
            dma((HALVES, n)),
            dma,
            dma,
            dma,
            dma,
        ],
        compiler_params=pltpu.CompilerParams(
            collective_id=0, has_side_effects=True, vmem_limit_bytes=56 * 1024 * 1024
        ),
    )(
        tokens,
        out_grad,
        expert_ids.T,
        gate_weights.T,
        w_gate,
        w_up,
        in_proj.transpose(0, 2, 1),
        out_proj.T,
    )


def solution(mesh):
    placed = (
        P(("groups", "expert"), None),
        P(("groups", "expert"), None),
        P(("groups", "expert"), None),
        P(("groups", "expert"), None),
        P("expert", None, None),
        P("expert", None, None),
        P("expert", None, None),
        P(),
    )
    return jax.shard_map(
        on_device,
        mesh=mesh,
        in_specs=placed,
        out_specs=P(("groups", "expert"), None),
        check_vma=False,
    )
```

```python
import functools
import jax
import jax.numpy as jnp
from jax import lax
from jax.experimental import pallas as pl
from jax.experimental.pallas import tpu as pltpu
from jax.sharding import PartitionSpec as P

STRIPES = 8
EX_LEN = 512
CAPACITY = 8
PIECES = 2
ORDER = (1, 0)
DIAGONAL_BY_FAR = (0,)
BF16 = jnp.bfloat16
F32 = jnp.float32
BY_LAST = (((1,), (1,)), ((), ()))


def toggled(m, bit):
    size = 1 << bit
    return m + size - 2 * size * lax.rem(lax.div(m, size), 2)


def kernel(
    n,
    tokens,
    out_grad,
    ids_hbm,
    gates_hbm,
    w_gate,
    w_up,
    in_proj,
    out_proj,
    out,
    tok,
    og,
    ids,
    gw,
    wg,
    wu,
    ip,
    op,
    outgoing,
    rows,
    grads_out,
    grads_in,
    sums_out,
    sums_in,
    load_sem,
    local_sem,
    send_sem,
    recv_sem,
    gsend_sem,
    grecv_sem,
    ssend_sem,
    srecv_sem,
):
    flight = n // STRIPES
    me = lax.axis_index("expert")
    octet, member = lax.div(me, STRIPES), lax.rem(me, STRIPES)
    base = octet * STRIPES
    width = tok.shape[1]
    tok_rows = tok.shape[0]
    rank = op.shape[0]
    part = rows.shape[3]

    loads = [
        pltpu.make_async_copy(src, dst, load_sem.at[i])
        for i, (src, dst) in enumerate(
            (
                (ids_hbm, ids),
                (gates_hbm, gw),
                (tokens, tok),
                (out_grad, og),
                (out_proj, op),
                (in_proj.at[0], ip),
                (w_gate.at[0], wg),
                (w_up.at[0], wu),
            )
        )
    ]
    for load in loads:
        load.start()

    barrier = pltpu.get_barrier_semaphore()

    def greet(target):
        pl.semaphore_signal(barrier, inc=1, device_id={"expert": target})

    def greet_across(step, carry):
        greet(lax.rem(octet + step, flight) * STRIPES + member)
        return carry

    lax.fori_loop(1, flight, greet_across, 0)
    for step in range(1, STRIPES):
        greet(base + lax.rem(member + step, STRIPES))

    loads[0].wait()
    loads[1].wait()
    used = flight * CAPACITY
    line = lax.broadcasted_iota(jnp.int32, (used, tok_rows), 0)
    expert_of, slot_of = lax.div(line, CAPACITY), lax.rem(line, CAPACITY)
    routed = jnp.zeros((used, tok_rows), F32)
    weight = jnp.zeros((used, tok_rows), F32)
    for k in range(ids.shape[0]):
        match = ids[k : k + 1] == expert_of
        routed = jnp.where(match, 1.0, routed)
        weight = weight + jnp.where(match, gw[k : k + 1], 0.0)
    upto = lax.broadcasted_iota(jnp.int32, (tok_rows, tok_rows), 0) <= lax.broadcasted_iota(
        jnp.int32, (tok_rows, tok_rows), 1
    )
    ranks = jnp.dot(
        routed.astype(BF16), jnp.where(upto, 1.0, 0.0).astype(BF16), preferred_element_type=F32
    )
    taken = (routed > 0.0) & (ranks == (slot_of + 1).astype(F32))
    sel = jnp.where(taken, 1.0, 0.0).astype(BF16)
    slot_weight = jnp.sum(jnp.where(taken, weight, 0.0), axis=1, keepdims=True)

    loads[2].wait()
    half = width // 2
    for h in range(PIECES):
        lo = h * part
        left = jnp.dot(sel, tok[:, lo : lo + part], preferred_element_type=F32)
        right = jnp.dot(sel, tok[:, half + lo : half + lo + part], preferred_element_type=F32)
        for e in range(flight):
            at = slice(e * CAPACITY, (e + 1) * CAPACITY)
            outgoing[h, e] = jnp.concatenate([left[at], right[at]], axis=0).astype(BF16)

    pl.semaphore_wait(barrier, flight - 1 + STRIPES - 1)

    def send(src, source, h, target):
        pltpu.make_async_remote_copy(
            src_ref=src,
            dst_ref=rows.at[h, source],
            send_sem=send_sem,
            recv_sem=recv_sem.at[h, source],
            device_id={"expert": target},
        ).start()

    def arrived(source, h):
        pltpu.make_async_copy(
            rows.at[h, source], rows.at[h, source], recv_sem.at[h, source]
        ).wait()

    core, near, far = (base + toggled(member, bit) for bit in range(3))

    def across(step, carry):
        e = lax.rem(octet + step, flight)
        for h in ORDER:
            send(outgoing.at[h, e], me, h, e * STRIPES + member)
        return carry

    lax.fori_loop(1, flight, across, 0)
    own = []
    for h in ORDER:
        for target in (far, near, core):
            send(outgoing.at[h, octet], me, h, target)
        keep = pltpu.make_async_copy(outgoing.at[h, octet], rows.at[h, me], local_sem.at[h])
        keep.start()
        own.append(keep)

    loads[3].wait()
    loads[4].wait()
    chosen = jnp.dot(sel, og[...], preferred_element_type=F32).astype(BF16)
    projected = lax.dot_general(chosen, op[...], BY_LAST, preferred_element_type=F32)
    weighted = (slot_weight * projected).astype(BF16).astype(F32)
    weighted = jnp.concatenate([weighted, jnp.zeros_like(weighted)], axis=1)
    for e in range(flight):
        grads_out[e] = weighted[e * CAPACITY : (e + 1) * CAPACITY]

    def send_grads(step, carry):
        e = lax.rem(octet + step, flight)
        pltpu.make_async_remote_copy(
            src_ref=grads_out.at[e],
            dst_ref=grads_in.at[member, octet],
            send_sem=gsend_sem.at[0],
            recv_sem=grecv_sem.at[0],
            device_id={"expert": e * STRIPES + member},
        ).start()
        return carry

    lax.fori_loop(1, flight, send_grads, 0)
    grads_in[member, octet] = grads_out[octet]

    def spread_grads():
        if flight > 1:
            some = grads_in.at[0, pl.ds(0, flight - 1)]
            pltpu.make_async_copy(some, some, grecv_sem.at[0]).wait()
        for step in range(1, STRIPES):
            pltpu.make_async_remote_copy(
                src_ref=grads_in.at[member],
                dst_ref=grads_in.at[member],
                send_sem=gsend_sem.at[1],
                recv_sem=grecv_sem.at[1],
                device_id={"expert": base + lax.rem(member + step, STRIPES)},
            ).start()

    def spread(at):
        near_source, far_source = at + toggled(member, 1), at + toggled(member, 2)
        for h in ORDER:
            arrived(far_source, h)
            if h not in DIAGONAL_BY_FAR:
                send(rows.at[h, far_source], far_source, h, near)
            send(rows.at[h, far_source], far_source, h, core)
            arrived(near_source, h)
            if h in DIAGONAL_BY_FAR:
                send(rows.at[h, near_source], near_source, h, far)
            send(rows.at[h, near_source], near_source, h, core)

    def finish(at):
        diagonal = at + toggled(toggled(member, 1), 2)
        for h in ORDER:
            arrived(diagonal, h)
            send(rows.at[h, diagonal], diagonal, h, core)

    def settle(at):
        for bits in ((), (1,), (2,), (1, 2)):
            source = toggled(member, 0)
            for bit in bits:
                source = toggled(source, bit)
            for h in range(PIECES):
                arrived(at + source, h)

    spread(base)

    def onward(step, carry):
        at = lax.rem(octet + step, flight) * STRIPES
        for h in ORDER:
            arrived(at + member, h)
            for target in (far, near, core):
                send(rows.at[h, at + member], at + member, h, target)
        return carry

    lax.fori_loop(1, flight, onward, 0)
    spread_grads()
    finish(base)

    loads[5].wait()
    examples_each = STRIPES * tok_rows // EX_LEN
    cols = examples_each * rank
    ip_wide = jnp.concatenate([ip[...]] * examples_each, axis=0)
    loads[6].wait()
    loads[7].wait()

    for keep in own:
        keep.wait()
    others = pl.ds(0, STRIPES - 1)
    pltpu.make_async_copy(grads_in.at[others], grads_in.at[others], grecv_sem.at[1]).wait()

    count = STRIPES * CAPACITY
    keep_cols = lax.div(
        lax.broadcasted_iota(jnp.int32, (count, cols), 0), EX_LEN // tok_rows * CAPACITY
    ) == lax.div(lax.broadcasted_iota(jnp.int32, (count, cols), 1), rank)

    def block(g):
        settle(g * STRIPES)
        sources = pl.ds(pl.multiple_of(g * STRIPES, STRIPES), STRIPES)
        gate = jnp.zeros((count, wg.shape[1]), F32)
        up = jnp.zeros((count, wg.shape[1]), F32)
        for h in range(PIECES):
            both = rows[h, sources].astype(F32)
            for side in range(2):
                x = both[:, side * CAPACITY : (side + 1) * CAPACITY].reshape(count, part)
                x = x.astype(BF16)
                lo = side * half + h * part
                gate = gate + jnp.dot(x, wg[lo : lo + part], preferred_element_type=F32)
                up = up + jnp.dot(x, wu[lo : lo + part], preferred_element_type=F32)
        hidden = (gate / (1.0 + jnp.exp(-gate)) * up).astype(BF16)
        inputs = lax.dot_general(hidden, ip_wide, BY_LAST, preferred_element_type=F32)
        inputs = jnp.where(keep_cols, inputs, 0.0)
        high = inputs.astype(BF16)
        rest_of = inputs - high.astype(F32)
        mid = rest_of.astype(BF16)
        low = (rest_of - mid.astype(F32)).astype(BF16)
        g_rows = grads_in[:, g].reshape(count, grads_in.shape[3]).astype(BF16)
        contract = (((0,), (0,)), ((), ()))
        total = lax.dot_general(
            jnp.concatenate([g_rows, g_rows, g_rows], axis=0),
            jnp.concatenate([low, mid, high], axis=0),
            contract,
            preferred_element_type=F32,
        )
        sums_out[:, :, pl.ds(pl.multiple_of(g * cols, cols), cols)] = total[:rank].reshape(
            STRIPES, rank // STRIPES, cols
        )

    def rest(step, carry):
        at = lax.rem(octet + step, flight) * STRIPES
        spread(at)
        block(lax.rem(octet + step - 1, flight))
        finish(at)
        return carry

    lax.fori_loop(1, flight, rest, 0)
    block(lax.rem(octet + flight - 1, flight))

    for step in range(1, STRIPES):
        target = lax.rem(member + step, STRIPES)
        pltpu.make_async_remote_copy(
            src_ref=sums_out.at[target],
            dst_ref=sums_in.at[member],
            send_sem=ssend_sem,
            recv_sem=srecv_sem,
            device_id={"expert": base + target},
        ).start()
    sums_in[member] = sums_out[member]
    pltpu.make_async_copy(
        rows.at[:, pl.ds(0, n - 1)], rows.at[:, pl.ds(0, n - 1)], send_sem
    ).wait()
    if flight > 1:
        some = grads_out.at[pl.ds(0, flight - 1)]
        pltpu.make_async_copy(some, some, gsend_sem.at[0]).wait()
    pltpu.make_async_copy(grads_in.at[others], grads_in.at[others], gsend_sem.at[1]).wait()
    pltpu.make_async_copy(sums_in.at[others], sums_in.at[others], srecv_sem).wait()
    total = sums_in[0]
    for j in range(1, STRIPES):
        total = total + sums_in[j]
    out[...] = total
    pltpu.make_async_copy(sums_in.at[others], sums_in.at[others], ssend_sem).wait()


def on_device(tokens, out_grad, expert_ids, gate_weights, w_gate, w_up, in_proj, out_proj):
    n = lax.axis_size("expert")
    flight = n // STRIPES
    tok_rows, width = tokens.shape
    hidden_units = w_gate.shape[2]
    rank = out_proj.shape[1]
    part = width // 2 // PIECES
    out_cols = n * tok_rows // EX_LEN * rank
    rank_each = rank // STRIPES
    dma = pltpu.SemaphoreType.DMA
    return pl.pallas_call(
        functools.partial(kernel, n),
        out_shape=jax.ShapeDtypeStruct((rank_each, out_cols), F32),
        in_specs=[pl.BlockSpec(memory_space=pl.ANY)] * 8,
        out_specs=pl.BlockSpec(memory_space=pltpu.VMEM),
        scratch_shapes=[
            pltpu.VMEM((tok_rows, width), BF16),
            pltpu.VMEM((tok_rows, width), BF16),
            pltpu.VMEM(expert_ids.shape[::-1], jnp.int32),
            pltpu.VMEM(gate_weights.shape[::-1], F32),
            pltpu.VMEM((width, hidden_units), BF16),
            pltpu.VMEM((width, hidden_units), BF16),
            pltpu.VMEM((rank, hidden_units), BF16),
            pltpu.VMEM((rank, width), BF16),
            pltpu.VMEM((PIECES, flight, 2 * CAPACITY, part), BF16),
            pltpu.VMEM((PIECES, n, 2 * CAPACITY, part), BF16),
            pltpu.VMEM((flight, CAPACITY, 2 * rank), F32),
            pltpu.VMEM((STRIPES, flight, CAPACITY, 2 * rank), F32),
            pltpu.VMEM((STRIPES, rank_each, out_cols), F32),
            pltpu.VMEM((STRIPES, rank_each, out_cols), F32),
            dma((8,)),
            dma((PIECES,)),
            dma,
            dma((PIECES, n)),
            dma((2,)),
            dma((2,)),
            dma,
            dma,
        ],
        compiler_params=pltpu.CompilerParams(
            collective_id=0, has_side_effects=True, vmem_limit_bytes=56 * 1024 * 1024
        ),
    )(
        tokens,
        out_grad,
        expert_ids.T,
        gate_weights.T,
        w_gate,
        w_up,
        in_proj.transpose(0, 2, 1),
        out_proj.T,
    )


def solution(mesh):
    placed = (
        P(("groups", "expert"), None),
        P(("groups", "expert"), None),
        P(("groups", "expert"), None),
        P(("groups", "expert"), None),
        P("expert", None, None),
        P("expert", None, None),
        P("expert", None, None),
        P(),
    )
    return jax.shard_map(
        on_device,
        mesh=mesh,
        in_specs=placed,
        out_specs=P(("groups", "expert"), None),
        check_vma=False,
    )
```

```python
import functools
import jax
import jax.numpy as jnp
from jax import lax
from jax.experimental import pallas as pl
from jax.experimental.pallas import tpu as pltpu
from jax.sharding import PartitionSpec as P

STRIPES = 8
EX_LEN = 512
CAPACITY = 8
PIECES = 2
ORDER = (1, 0)
BY_FAR_FIRST = ()
BY_FAR_LATER = (0,)
BF16 = jnp.bfloat16
F32 = jnp.float32
BY_LAST = (((1,), (1,)), ((), ()))


def toggled(m, bit):
    size = 1 << bit
    return m + size - 2 * size * lax.rem(lax.div(m, size), 2)


def kernel(
    n,
    tokens,
    out_grad,
    ids_hbm,
    gates_hbm,
    w_gate,
    w_up,
    in_proj,
    out_proj,
    out,
    tok,
    og,
    ids,
    gw,
    wg,
    wu,
    ip,
    op,
    outgoing,
    rows,
    grads_out,
    grads_in,
    sums_out,
    sums_in,
    load_sem,
    local_sem,
    send_sem,
    recv_sem,
    gsend_sem,
    grecv_sem,
    ssend_sem,
    srecv_sem,
):
    flight = n // STRIPES
    me = lax.axis_index("expert")
    octet, member = lax.div(me, STRIPES), lax.rem(me, STRIPES)
    base = octet * STRIPES
    width = tok.shape[1]
    tok_rows = tok.shape[0]
    rank = op.shape[0]
    part = rows.shape[3]

    loads = [
        pltpu.make_async_copy(src, dst, load_sem.at[i])
        for i, (src, dst) in enumerate(
            (
                (ids_hbm, ids),
                (gates_hbm, gw),
                (tokens, tok),
                (out_grad, og),
                (out_proj, op),
                (in_proj.at[0], ip),
                (w_gate.at[0], wg),
                (w_up.at[0], wu),
            )
        )
    ]
    for load in loads:
        load.start()

    barrier = pltpu.get_barrier_semaphore()

    def greet(target):
        pl.semaphore_signal(barrier, inc=1, device_id={"expert": target})

    def greet_across(step, carry):
        greet(lax.rem(octet + step, flight) * STRIPES + member)
        return carry

    lax.fori_loop(1, flight, greet_across, 0)
    for step in range(1, STRIPES):
        greet(base + lax.rem(member + step, STRIPES))

    loads[0].wait()
    loads[1].wait()
    used = flight * CAPACITY
    line = lax.broadcasted_iota(jnp.int32, (used, tok_rows), 0)
    expert_of, slot_of = lax.div(line, CAPACITY), lax.rem(line, CAPACITY)
    routed = jnp.zeros((used, tok_rows), F32)
    weight = jnp.zeros((used, tok_rows), F32)
    for k in range(ids.shape[0]):
        match = ids[k : k + 1] == expert_of
        routed = jnp.where(match, 1.0, routed)
        weight = weight + jnp.where(match, gw[k : k + 1], 0.0)
    upto = lax.broadcasted_iota(jnp.int32, (tok_rows, tok_rows), 0) <= lax.broadcasted_iota(
        jnp.int32, (tok_rows, tok_rows), 1
    )
    ranks = jnp.dot(
        routed.astype(BF16), jnp.where(upto, 1.0, 0.0).astype(BF16), preferred_element_type=F32
    )
    taken = (routed > 0.0) & (ranks == (slot_of + 1).astype(F32))
    sel = jnp.where(taken, 1.0, 0.0).astype(BF16)
    slot_weight = jnp.sum(jnp.where(taken, weight, 0.0), axis=1, keepdims=True)

    loads[2].wait()
    half = width // 2
    for h in range(PIECES):
        lo = h * part
        left = jnp.dot(sel, tok[:, lo : lo + part], preferred_element_type=F32)
        right = jnp.dot(sel, tok[:, half + lo : half + lo + part], preferred_element_type=F32)
        for e in range(flight):
            at = slice(e * CAPACITY, (e + 1) * CAPACITY)
            outgoing[h, e] = jnp.concatenate([left[at], right[at]], axis=0).astype(BF16)

    pl.semaphore_wait(barrier, flight - 1 + STRIPES - 1)

    def send(src, source, h, target):
        pltpu.make_async_remote_copy(
            src_ref=src,
            dst_ref=rows.at[h, source],
            send_sem=send_sem,
            recv_sem=recv_sem.at[h, source],
            device_id={"expert": target},
        ).start()

    def arrived(source, h):
        pltpu.make_async_copy(
            rows.at[h, source], rows.at[h, source], recv_sem.at[h, source]
        ).wait()

    core, near, far = (base + toggled(member, bit) for bit in range(3))

    def across(step, carry):
        e = lax.rem(octet + step, flight)
        for h in ORDER:
            send(outgoing.at[h, e], me, h, e * STRIPES + member)
        return carry

    lax.fori_loop(1, flight, across, 0)
    own = []
    for h in ORDER:
        for target in (far, near, core):
            send(outgoing.at[h, octet], me, h, target)
        keep = pltpu.make_async_copy(outgoing.at[h, octet], rows.at[h, me], local_sem.at[h])
        keep.start()
        own.append(keep)

    loads[3].wait()
    loads[4].wait()
    chosen = jnp.dot(sel, og[...], preferred_element_type=F32).astype(BF16)
    projected = lax.dot_general(chosen, op[...], BY_LAST, preferred_element_type=F32)
    weighted = (slot_weight * projected).astype(BF16).astype(F32)
    weighted = jnp.concatenate([weighted, jnp.zeros_like(weighted)], axis=1)
    for e in range(flight):
        grads_out[e] = weighted[e * CAPACITY : (e + 1) * CAPACITY]

    def send_grads(step, carry):
        e = lax.rem(octet + step, flight)
        pltpu.make_async_remote_copy(
            src_ref=grads_out.at[e],
            dst_ref=grads_in.at[member, octet],
            send_sem=gsend_sem.at[0],
            recv_sem=grecv_sem.at[0],
            device_id={"expert": e * STRIPES + member},
        ).start()
        return carry

    lax.fori_loop(1, flight, send_grads, 0)
    grads_in[member, octet] = grads_out[octet]

    def spread_grads():
        if flight > 1:
            some = grads_in.at[0, pl.ds(0, flight - 1)]
            pltpu.make_async_copy(some, some, grecv_sem.at[0]).wait()
        for step in range(1, STRIPES):
            pltpu.make_async_remote_copy(
                src_ref=grads_in.at[member],
                dst_ref=grads_in.at[member],
                send_sem=gsend_sem.at[1],
                recv_sem=grecv_sem.at[1],
                device_id={"expert": base + lax.rem(member + step, STRIPES)},
            ).start()

    def spread(at, by_far):
        near_source, far_source = at + toggled(member, 1), at + toggled(member, 2)
        for h in ORDER:
            arrived(far_source, h)
            if h not in by_far:
                send(rows.at[h, far_source], far_source, h, near)
            send(rows.at[h, far_source], far_source, h, core)
            arrived(near_source, h)
            if h in by_far:
                send(rows.at[h, near_source], near_source, h, far)
            send(rows.at[h, near_source], near_source, h, core)

    def finish(at):
        diagonal = at + toggled(toggled(member, 1), 2)
        for h in ORDER:
            arrived(diagonal, h)
            send(rows.at[h, diagonal], diagonal, h, core)

    def settle(at, h):
        for bits in ((), (1,), (2,), (1, 2)):
            source = toggled(member, 0)
            for bit in bits:
                source = toggled(source, bit)
            arrived(at + source, h)

    spread(base, BY_FAR_FIRST)

    def onward(step, carry):
        at = lax.rem(octet + step, flight) * STRIPES
        for h in ORDER:
            arrived(at + member, h)
            for target in (far, near, core):
                send(rows.at[h, at + member], at + member, h, target)
        return carry

    lax.fori_loop(1, flight, onward, 0)
    spread_grads()
    finish(base)

    loads[5].wait()
    examples_each = STRIPES * tok_rows // EX_LEN
    cols = examples_each * rank
    ip_wide = jnp.concatenate([ip[...]] * examples_each, axis=0)
    loads[6].wait()
    loads[7].wait()

    for keep in own:
        keep.wait()
    others = pl.ds(0, STRIPES - 1)
    pltpu.make_async_copy(grads_in.at[others], grads_in.at[others], grecv_sem.at[1]).wait()

    count = STRIPES * CAPACITY
    keep_cols = lax.div(
        lax.broadcasted_iota(jnp.int32, (count, cols), 0), EX_LEN // tok_rows * CAPACITY
    ) == lax.div(lax.broadcasted_iota(jnp.int32, (count, cols), 1), rank)

    def block(g):
        sources = pl.ds(pl.multiple_of(g * STRIPES, STRIPES), STRIPES)
        gate = jnp.zeros((count, wg.shape[1]), F32)
        up = jnp.zeros((count, wg.shape[1]), F32)
        for h in ORDER:
            settle(g * STRIPES, h)
            both = rows[h, sources].astype(F32)
            for side in range(2):
                x = both[:, side * CAPACITY : (side + 1) * CAPACITY].reshape(count, part)
                x = x.astype(BF16)
                lo = side * half + h * part
                gate = gate + jnp.dot(x, wg[lo : lo + part], preferred_element_type=F32)
                up = up + jnp.dot(x, wu[lo : lo + part], preferred_element_type=F32)
        hidden = (gate / (1.0 + jnp.exp(-gate)) * up).astype(BF16)
        inputs = lax.dot_general(hidden, ip_wide, BY_LAST, preferred_element_type=F32)
        inputs = jnp.where(keep_cols, inputs, 0.0)
        high = inputs.astype(BF16)
        rest_of = inputs - high.astype(F32)
        mid = rest_of.astype(BF16)
        low = (rest_of - mid.astype(F32)).astype(BF16)
        g_rows = grads_in[:, g].reshape(count, grads_in.shape[3]).astype(BF16)
        contract = (((0,), (0,)), ((), ()))
        total = lax.dot_general(
            jnp.concatenate([g_rows, g_rows, g_rows], axis=0),
            jnp.concatenate([low, mid, high], axis=0),
            contract,
            preferred_element_type=F32,
        )
        sums_out[:, :, pl.ds(pl.multiple_of(g * cols, cols), cols)] = total[:rank].reshape(
            STRIPES, rank // STRIPES, cols
        )

    def rest(step, carry):
        at = lax.rem(octet + step, flight) * STRIPES
        spread(at, BY_FAR_LATER)
        block(lax.rem(octet + step - 1, flight))
        finish(at)
        return carry

    lax.fori_loop(1, flight, rest, 0)
    block(lax.rem(octet + flight - 1, flight))

    for step in range(1, STRIPES):
        target = lax.rem(member + step, STRIPES)
        pltpu.make_async_remote_copy(
            src_ref=sums_out.at[target],
            dst_ref=sums_in.at[member],
            send_sem=ssend_sem,
            recv_sem=srecv_sem,
            device_id={"expert": base + target},
        ).start()
    sums_in[member] = sums_out[member]
    pltpu.make_async_copy(
        rows.at[:, pl.ds(0, n - 1)], rows.at[:, pl.ds(0, n - 1)], send_sem
    ).wait()
    if flight > 1:
        some = grads_out.at[pl.ds(0, flight - 1)]
        pltpu.make_async_copy(some, some, gsend_sem.at[0]).wait()
    pltpu.make_async_copy(grads_in.at[others], grads_in.at[others], gsend_sem.at[1]).wait()
    pltpu.make_async_copy(sums_in.at[others], sums_in.at[others], srecv_sem).wait()
    total = sums_in[0]
    for j in range(1, STRIPES):
        total = total + sums_in[j]
    out[...] = total
    pltpu.make_async_copy(sums_in.at[others], sums_in.at[others], ssend_sem).wait()


def on_device(tokens, out_grad, expert_ids, gate_weights, w_gate, w_up, in_proj, out_proj):
    n = lax.axis_size("expert")
    flight = n // STRIPES
    tok_rows, width = tokens.shape
    hidden_units = w_gate.shape[2]
    rank = out_proj.shape[1]
    part = width // 2 // PIECES
    out_cols = n * tok_rows // EX_LEN * rank
    rank_each = rank // STRIPES
    dma = pltpu.SemaphoreType.DMA
    return pl.pallas_call(
        functools.partial(kernel, n),
        out_shape=jax.ShapeDtypeStruct((rank_each, out_cols), F32),
        in_specs=[pl.BlockSpec(memory_space=pl.ANY)] * 8,
        out_specs=pl.BlockSpec(memory_space=pltpu.VMEM),
        scratch_shapes=[
            pltpu.VMEM((tok_rows, width), BF16),
            pltpu.VMEM((tok_rows, width), BF16),
            pltpu.VMEM(expert_ids.shape[::-1], jnp.int32),
            pltpu.VMEM(gate_weights.shape[::-1], F32),
            pltpu.VMEM((width, hidden_units), BF16),
            pltpu.VMEM((width, hidden_units), BF16),
            pltpu.VMEM((rank, hidden_units), BF16),
            pltpu.VMEM((rank, width), BF16),
            pltpu.VMEM((PIECES, flight, 2 * CAPACITY, part), BF16),
            pltpu.VMEM((PIECES, n, 2 * CAPACITY, part), BF16),
            pltpu.VMEM((flight, CAPACITY, 2 * rank), F32),
            pltpu.VMEM((STRIPES, flight, CAPACITY, 2 * rank), F32),
            pltpu.VMEM((STRIPES, rank_each, out_cols), F32),
            pltpu.VMEM((STRIPES, rank_each, out_cols), F32),
            dma((8,)),
            dma((PIECES,)),
            dma,
            dma((PIECES, n)),
            dma((2,)),
            dma((2,)),
            dma,
            dma,
        ],
        compiler_params=pltpu.CompilerParams(
            collective_id=0, has_side_effects=True, vmem_limit_bytes=56 * 1024 * 1024
        ),
    )(
        tokens,
        out_grad,
        expert_ids.T,
        gate_weights.T,
        w_gate,
        w_up,
        in_proj.transpose(0, 2, 1),
        out_proj.T,
    )


def solution(mesh):
    placed = (
        P(("groups", "expert"), None),
        P(("groups", "expert"), None),
        P(("groups", "expert"), None),
        P(("groups", "expert"), None),
        P("expert", None, None),
        P("expert", None, None),
        P("expert", None, None),
        P(),
    )
    return jax.shard_map(
        on_device,
        mesh=mesh,
        in_specs=placed,
        out_specs=P(("groups", "expert"), None),
        check_vma=False,
    )
```

```python
import functools
import jax
import jax.numpy as jnp
from jax import lax
from jax.experimental import pallas as pl
from jax.experimental.pallas import tpu as pltpu
from jax.sharding import PartitionSpec as P

STRIPES = 8
EX_LEN = 512
CAPACITY = 8
PIECES = 2
ORDER = (1, 0)
BY_FAR_FIRST = ()
BY_FAR_LATER = (0,)
BF16 = jnp.bfloat16
F32 = jnp.float32
BY_LAST = (((1,), (1,)), ((), ()))


def toggled(m, bit):
    size = 1 << bit
    return m + size - 2 * size * lax.rem(lax.div(m, size), 2)


def kernel(
    n,
    tokens,
    out_grad,
    ids_hbm,
    gates_hbm,
    w_gate,
    w_up,
    in_proj,
    out_proj,
    out,
    tok,
    og,
    ids,
    gw,
    wg,
    wu,
    ip,
    op,
    outgoing,
    rows,
    grads_out,
    grads_in,
    sums_out,
    sums_in,
    load_sem,
    local_sem,
    send_sem,
    recv_sem,
    gsend_sem,
    grecv_sem,
    ssend_sem,
    srecv_sem,
):
    flight = n // STRIPES
    me = lax.axis_index("expert")
    octet, member = lax.div(me, STRIPES), lax.rem(me, STRIPES)
    base = octet * STRIPES
    width = tok.shape[1]
    tok_rows = tok.shape[0]
    rank = op.shape[0]
    part = rows.shape[3]

    loads = [
        pltpu.make_async_copy(src, dst, load_sem.at[i])
        for i, (src, dst) in enumerate(
            (
                (ids_hbm, ids),
                (gates_hbm, gw),
                (tokens, tok),
                (out_grad, og),
                (out_proj, op),
                (in_proj.at[0], ip),
                (w_gate.at[0], wg),
                (w_up.at[0], wu),
            )
        )
    ]
    for load in loads:
        load.start()

    barrier = pltpu.get_barrier_semaphore()

    def greet(target):
        pl.semaphore_signal(barrier, inc=1, device_id={"expert": target})

    def greet_across(step, carry):
        greet(lax.rem(octet + step, flight) * STRIPES + member)
        return carry

    lax.fori_loop(1, flight, greet_across, 0)
    for step in range(1, STRIPES):
        greet(base + lax.rem(member + step, STRIPES))

    loads[0].wait()
    loads[1].wait()
    used = flight * CAPACITY
    line = lax.broadcasted_iota(jnp.int32, (used, tok_rows), 0)
    expert_of, slot_of = lax.div(line, CAPACITY), lax.rem(line, CAPACITY)
    routed = jnp.zeros((used, tok_rows), F32)
    weight = jnp.zeros((used, tok_rows), F32)
    for k in range(ids.shape[0]):
        match = ids[k : k + 1] == expert_of
        routed = jnp.where(match, 1.0, routed)
        weight = weight + jnp.where(match, gw[k : k + 1], 0.0)
    upto = lax.broadcasted_iota(jnp.int32, (tok_rows, tok_rows), 0) <= lax.broadcasted_iota(
        jnp.int32, (tok_rows, tok_rows), 1
    )
    ranks = jnp.dot(
        routed.astype(BF16), jnp.where(upto, 1.0, 0.0).astype(BF16), preferred_element_type=F32
    )
    taken = (routed > 0.0) & (ranks == (slot_of + 1).astype(F32))
    sel = jnp.where(taken, 1.0, 0.0).astype(BF16)
    slot_weight = jnp.sum(jnp.where(taken, weight, 0.0), axis=1, keepdims=True)

    loads[2].wait()
    half = width // 2
    pl.semaphore_wait(barrier, flight - 1 + STRIPES - 1)

    def send(src, source, h, target):
        pltpu.make_async_remote_copy(
            src_ref=src,
            dst_ref=rows.at[h, source],
            send_sem=send_sem,
            recv_sem=recv_sem.at[h, source],
            device_id={"expert": target},
        ).start()

    def arrived(source, h):
        pltpu.make_async_copy(
            rows.at[h, source], rows.at[h, source], recv_sem.at[h, source]
        ).wait()

    core, near, far = (base + toggled(member, bit) for bit in range(3))

    own = []
    for h in ORDER:
        lo = h * part
        left = jnp.dot(sel, tok[:, lo : lo + part], preferred_element_type=F32)
        right = jnp.dot(sel, tok[:, half + lo : half + lo + part], preferred_element_type=F32)
        for e in range(flight):
            at = slice(e * CAPACITY, (e + 1) * CAPACITY)
            outgoing[h, e] = jnp.concatenate([left[at], right[at]], axis=0).astype(BF16)

        def across(step, carry):
            e = lax.rem(octet + step, flight)
            send(outgoing.at[h, e], me, h, e * STRIPES + member)
            return carry

        lax.fori_loop(1, flight, across, 0)
        for target in (far, near, core):
            send(outgoing.at[h, octet], me, h, target)
        keep = pltpu.make_async_copy(outgoing.at[h, octet], rows.at[h, me], local_sem.at[h])
        keep.start()
        own.append(keep)

    loads[3].wait()
    loads[4].wait()
    chosen = jnp.dot(sel, og[...], preferred_element_type=F32).astype(BF16)
    projected = lax.dot_general(chosen, op[...], BY_LAST, preferred_element_type=F32)
    weighted = (slot_weight * projected).astype(BF16).astype(F32)
    weighted = jnp.concatenate([weighted, jnp.zeros_like(weighted)], axis=1)
    for e in range(flight):
        grads_out[e] = weighted[e * CAPACITY : (e + 1) * CAPACITY]

    def send_grads(step, carry):
        e = lax.rem(octet + step, flight)
        pltpu.make_async_remote_copy(
            src_ref=grads_out.at[e],
            dst_ref=grads_in.at[member, octet],
            send_sem=gsend_sem.at[0],
            recv_sem=grecv_sem.at[0],
            device_id={"expert": e * STRIPES + member},
        ).start()
        return carry

    lax.fori_loop(1, flight, send_grads, 0)
    grads_in[member, octet] = grads_out[octet]

    def spread_grads():
        if flight > 1:
            some = grads_in.at[0, pl.ds(0, flight - 1)]
            pltpu.make_async_copy(some, some, grecv_sem.at[0]).wait()
        for step in range(1, STRIPES):
            pltpu.make_async_remote_copy(
                src_ref=grads_in.at[member],
                dst_ref=grads_in.at[member],
                send_sem=gsend_sem.at[1],
                recv_sem=grecv_sem.at[1],
                device_id={"expert": base + lax.rem(member + step, STRIPES)},
            ).start()

    def spread(at, by_far):
        near_source, far_source = at + toggled(member, 1), at + toggled(member, 2)
        for h in ORDER:
            arrived(far_source, h)
            if h not in by_far:
                send(rows.at[h, far_source], far_source, h, near)
            send(rows.at[h, far_source], far_source, h, core)
            arrived(near_source, h)
            if h in by_far:
                send(rows.at[h, near_source], near_source, h, far)
            send(rows.at[h, near_source], near_source, h, core)

    def finish(at):
        diagonal = at + toggled(toggled(member, 1), 2)
        for h in ORDER:
            arrived(diagonal, h)
            send(rows.at[h, diagonal], diagonal, h, core)

    def settle(at, h):
        for bits in ((), (1,), (2,), (1, 2)):
            source = toggled(member, 0)
            for bit in bits:
                source = toggled(source, bit)
            arrived(at + source, h)

    spread(base, BY_FAR_FIRST)

    def onward(step, carry):
        at = lax.rem(octet + step, flight) * STRIPES
        for h in ORDER:
            arrived(at + member, h)
            for target in (far, near, core):
                send(rows.at[h, at + member], at + member, h, target)
        return carry

    lax.fori_loop(1, flight, onward, 0)
    spread_grads()
    finish(base)

    loads[5].wait()
    examples_each = STRIPES * tok_rows // EX_LEN
    cols = examples_each * rank
    ip_wide = jnp.concatenate([ip[...]] * examples_each, axis=0)
    loads[6].wait()
    loads[7].wait()

    for keep in own:
        keep.wait()
    others = pl.ds(0, STRIPES - 1)
    pltpu.make_async_copy(grads_in.at[others], grads_in.at[others], grecv_sem.at[1]).wait()

    count = STRIPES * CAPACITY
    keep_cols = lax.div(
        lax.broadcasted_iota(jnp.int32, (count, cols), 0), EX_LEN // tok_rows * CAPACITY
    ) == lax.div(lax.broadcasted_iota(jnp.int32, (count, cols), 1), rank)

    def block(g):
        sources = pl.ds(pl.multiple_of(g * STRIPES, STRIPES), STRIPES)
        gate = jnp.zeros((count, wg.shape[1]), F32)
        up = jnp.zeros((count, wg.shape[1]), F32)
        for h in ORDER:
            settle(g * STRIPES, h)
            both = rows[h, sources].astype(F32)
            for side in range(2):
                x = both[:, side * CAPACITY : (side + 1) * CAPACITY].reshape(count, part)
                x = x.astype(BF16)
                lo = side * half + h * part
                gate = gate + jnp.dot(x, wg[lo : lo + part], preferred_element_type=F32)
                up = up + jnp.dot(x, wu[lo : lo + part], preferred_element_type=F32)
        hidden = (gate / (1.0 + jnp.exp(-gate)) * up).astype(BF16)
        inputs = lax.dot_general(hidden, ip_wide, BY_LAST, preferred_element_type=F32)
        inputs = jnp.where(keep_cols, inputs, 0.0)
        high = inputs.astype(BF16)
        rest_of = inputs - high.astype(F32)
        mid = rest_of.astype(BF16)
        low = (rest_of - mid.astype(F32)).astype(BF16)
        g_rows = grads_in[:, g].reshape(count, grads_in.shape[3]).astype(BF16)
        contract = (((0,), (0,)), ((), ()))
        total = lax.dot_general(
            jnp.concatenate([g_rows, g_rows, g_rows], axis=0),
            jnp.concatenate([low, mid, high], axis=0),
            contract,
            preferred_element_type=F32,
        )
        sums_out[:, :, pl.ds(pl.multiple_of(g * cols, cols), cols)] = total[:rank].reshape(
            STRIPES, rank // STRIPES, cols
        )

    def rest(step, carry):
        at = lax.rem(octet + step, flight) * STRIPES
        spread(at, BY_FAR_LATER)
        block(lax.rem(octet + step - 1, flight))
        finish(at)
        return carry

    lax.fori_loop(1, flight, rest, 0)
    block(lax.rem(octet + flight - 1, flight))

    for step in range(1, STRIPES):
        target = lax.rem(member + step, STRIPES)
        pltpu.make_async_remote_copy(
            src_ref=sums_out.at[target],
            dst_ref=sums_in.at[member],
            send_sem=ssend_sem,
            recv_sem=srecv_sem,
            device_id={"expert": base + target},
        ).start()
    sums_in[member] = sums_out[member]
    pltpu.make_async_copy(
        rows.at[:, pl.ds(0, n - 1)], rows.at[:, pl.ds(0, n - 1)], send_sem
    ).wait()
    if flight > 1:
        some = grads_out.at[pl.ds(0, flight - 1)]
        pltpu.make_async_copy(some, some, gsend_sem.at[0]).wait()
    pltpu.make_async_copy(grads_in.at[others], grads_in.at[others], gsend_sem.at[1]).wait()
    pltpu.make_async_copy(sums_in.at[others], sums_in.at[others], srecv_sem).wait()
    total = sums_in[0]
    for j in range(1, STRIPES):
        total = total + sums_in[j]
    out[...] = total
    pltpu.make_async_copy(sums_in.at[others], sums_in.at[others], ssend_sem).wait()


def on_device(tokens, out_grad, expert_ids, gate_weights, w_gate, w_up, in_proj, out_proj):
    n = lax.axis_size("expert")
    flight = n // STRIPES
    tok_rows, width = tokens.shape
    hidden_units = w_gate.shape[2]
    rank = out_proj.shape[1]
    part = width // 2 // PIECES
    out_cols = n * tok_rows // EX_LEN * rank
    rank_each = rank // STRIPES
    dma = pltpu.SemaphoreType.DMA
    return pl.pallas_call(
        functools.partial(kernel, n),
        out_shape=jax.ShapeDtypeStruct((rank_each, out_cols), F32),
        in_specs=[pl.BlockSpec(memory_space=pl.ANY)] * 8,
        out_specs=pl.BlockSpec(memory_space=pltpu.VMEM),
        scratch_shapes=[
            pltpu.VMEM((tok_rows, width), BF16),
            pltpu.VMEM((tok_rows, width), BF16),
            pltpu.VMEM(expert_ids.shape[::-1], jnp.int32),
            pltpu.VMEM(gate_weights.shape[::-1], F32),
            pltpu.VMEM((width, hidden_units), BF16),
            pltpu.VMEM((width, hidden_units), BF16),
            pltpu.VMEM((rank, hidden_units), BF16),
            pltpu.VMEM((rank, width), BF16),
            pltpu.VMEM((PIECES, flight, 2 * CAPACITY, part), BF16),
            pltpu.VMEM((PIECES, n, 2 * CAPACITY, part), BF16),
            pltpu.VMEM((flight, CAPACITY, 2 * rank), F32),
            pltpu.VMEM((STRIPES, flight, CAPACITY, 2 * rank), F32),
            pltpu.VMEM((STRIPES, rank_each, out_cols), F32),
            pltpu.VMEM((STRIPES, rank_each, out_cols), F32),
            dma((8,)),
            dma((PIECES,)),
            dma,
            dma((PIECES, n)),
            dma((2,)),
            dma((2,)),
            dma,
            dma,
        ],
        compiler_params=pltpu.CompilerParams(
            collective_id=0, has_side_effects=True, vmem_limit_bytes=56 * 1024 * 1024
        ),
    )(
        tokens,
        out_grad,
        expert_ids.T,
        gate_weights.T,
        w_gate,
        w_up,
        in_proj.transpose(0, 2, 1),
        out_proj.T,
    )


def solution(mesh):
    placed = (
        P(("groups", "expert"), None),
        P(("groups", "expert"), None),
        P(("groups", "expert"), None),
        P(("groups", "expert"), None),
        P("expert", None, None),
        P("expert", None, None),
        P("expert", None, None),
        P(),
    )
    return jax.shard_map(
        on_device,
        mesh=mesh,
        in_specs=placed,
        out_specs=P(("groups", "expert"), None),
        check_vma=False,
    )
```
